32 devices in a mesh: node: 4 (over z), local: 8 (over y, x, core).
Axes of the slice: x: 2, y: 2, z: 4, core: 2. Of those that a mesh axis runs over, the one named last changes fastest.
Arguments:
- tokens: bfloat16 [4096, 4096], P(('node', 'local')), may hold values from -6 to 6
- cotangent: bfloat16 [4096, 4096], P(('node', 'local')), may hold values from -6 to 6
- gate_probs: float32 [4096, 8], P(('node', 'local')), may hold values from 0.02 to 0.5
- experts: int32 [4096, 8], P(('node', 'local')), may hold values from 0 to 31, all different within a row; in each aligned block of 128 rows (0 to 127, 128 to 255, ...) at most 40 rows name the same one
- stratum: int32 [32], P(('node', 'local')), may hold values from 0 to 7
- token_level: int32 [4096], P(('node', 'local')), may hold values from 0 to 63
- w_gate_up: bfloat16 [32, 4096, 1024], P(('node', 'local')), may hold values from -0.09375 to 0.09375
- w_down: bfloat16 [32, 512, 4096], P(('node', 'local')), may hold values from -0.25 to 0.25
Outputs:
- grad_tokens: bfloat16 [4096, 4096], P(('node', 'local'))
- grad_probs: bfloat16 [4096, 8], P(('node', 'local'))
The draws below stay inside these ranges and needn't reach their ends.
Inputs may be any that keep to these rules, and one draw needn't show every extreme that they name: Among the tokens of one device no expert is named more than 40 times; in every draw some expert is named exactly 40 times by the tokens of some device. A token names 8 different experts.
All inputs are finite; a program needn't handle non-finite values.
Results may differ from the reference program's by a relative error of at most 0.013.
Values may be sent and summed in bfloat16 or wider, within the bound.
A program may use at most 192 MiB of HBM per device.

```python
import math
import jax
import jax.numpy as jnp
import numpy as np
from jax import lax

D = 4096
H = 512
TOP = 8
STRATA = 8
LEVELS = 64
TOK_DEV = 128
EXPERTS = 32
TOKENS = 4096
CAP = 40
N_NODE = 4
N_LOCAL = 8


def with_ends(entries, key, smallest, largest):
    extent = entries.shape
    place = [jax.random.randint(jax.random.fold_in(key, axis), (), 0, extent[axis]) for axis in range(len(extent))]
    entries = entries.at[tuple(place)].set(smallest)
    longest = extent.index(max(extent))
    place[longest] = (place[longest] + 1) % extent[longest]
    return entries.at[tuple(place)].set(largest)


def block_scale(rng, dims, split, smallest, top_value):
    level = 1.0
    for dim, blocks in split:
        draws = jax.random.uniform(jax.random.fold_in(jax.random.fold_in(rng, 6), dim), (blocks,), jnp.float32, smallest / len(split), top_value / len(split))
        level = level * jnp.repeat(jnp.exp(draws), dims[dim] // blocks).reshape((-1,) + (1,) * (len(dims) - 1 - dim))
    return level


def assign_block(stream_key, own, number, rows, number_of, top, most, lean):
    sequence = jax.random.permutation(stream_key, number_of)
    crowded, usual = shares(number_of, rows * top, most, lean, True), shares(number_of, rows * top, most, lean, False)
    places = jnp.arange(number_of)

    def named(lengths, rotation):
        used = int((lengths > 0).sum())
        fixed = max(1, used // 4)
        passed = fixed + (places - fixed + rotation * (used - fixed)) % max(1, number_of - fixed)
        return jnp.zeros((number_of,), jnp.int32).at[sequence[jnp.where(places < fixed, places, passed)]].set(jnp.asarray(lengths, jnp.int32))

    lengths = jnp.where(number % 4 == 0, named(crowded, number // 4), named(usual, number - number // 4 - 1))
    mixed = jax.random.permutation(jax.random.fold_in(own, 3), number_of)
    giver, receiver = mixed[0:number_of // 2 * 2:2], mixed[1:number_of // 2 * 2:2]
    margin = jnp.minimum(lengths[giver] - 1, most - lengths[receiver]) // 2
    margin = jnp.where((giver == sequence[0]) | (receiver == sequence[0]) | (lengths[receiver] == 0), 0, jnp.maximum(margin, 0))
    passed = jax.random.randint(jax.random.fold_in(own, 4), (number_of // 2,), 0, 1 << 20) % (margin + 1)
    lengths = lengths.at[giver].add(-passed).at[receiver].add(passed)
    members = jnp.searchsorted(jnp.cumsum(lengths), jnp.arange(rows * top), side="right").astype(jnp.int32)
    table = members.reshape(top, rows).T
    table = table[jax.random.permutation(jax.random.fold_in(own, 1), rows)]
    rotation = jax.random.randint(jax.random.fold_in(own, 2), (rows, 1), 0, top)
    return jnp.take_along_axis(table, (jnp.arange(top)[None, :] + rotation) % top, axis=1)


def shares(amount, total, reach, lean, full):
    weights = [(1 << 20) // math.isqrt(rank ** lean) + 1 for rank in range(1, amount + 1)]
    largest = reach if full else min(reach, max(-(-total // amount), total * weights[0] // sum(weights)))
    least = 1 if total - largest >= amount - 1 else 0
    given, spare = [largest] + [least] * (amount - 1), total - largest - least * (amount - 1)
    while spare > 0:
        candidates = [i for i in range(1, amount) if given[i] < largest] or [i for i in range(1, amount) if given[i] < reach]
        whole, remaining = sum([weights[i] for i in candidates]), spare
        for i in candidates:
            extra = min(reach - given[i], max(1, remaining * weights[i] // whole), spare)
            given[i] = given[i] + extra
            spare = spare - extra
    return np.array(given)


def scatter_about(stream_key, extent, spread, most, cuts=(), held_as=jnp.bfloat16):
    entries = jax.random.normal(stream_key, extent, jnp.float32) * spread
    if len(cuts) > 0:
        entries = block_scale(stream_key, extent, cuts, -0.22, 0.18) * entries
    return jnp.clip(entries, min=-most, max=most).astype(held_as)


def setup_inputs(seed: int = 0) -> dict:
    keys = jax.random.split(jax.random.key(seed), 9)
    tokens = scatter_about(keys[0], (TOKENS, D), 1.0, 6.0, ((0, 32),))
    cotangent = scatter_about(keys[1], (TOKENS, D), 1.0, 6.0, ((0, 32),))
    gate_probs = jnp.clip(jnp.exp(math.log(0.5) - 3.218876 * jax.random.uniform(keys[2], (TOKENS, TOP), jnp.float32) ** block_scale(keys[2], (TOKENS, TOP), ((0, 32),), -0.2, 0.2)), 0.02, 0.5)
    experts_keys = jax.random.split(jax.random.fold_in(keys[3], 1), TOKENS // TOK_DEV)
    experts_turns = jax.random.permutation(jax.random.fold_in(keys[3], 3), TOKENS // TOK_DEV)
    experts = jax.vmap(lambda own, number: assign_block(jax.random.fold_in(keys[3], 2), own, number, TOK_DEV, EXPERTS, TOP, CAP, 2))(experts_keys, experts_turns).reshape((TOKENS, TOP))
    stratum = with_ends(jax.random.randint(keys[4], (N_NODE * N_LOCAL,), 0, STRATA), jax.random.fold_in(keys[4], 1), 0, STRATA - 1).astype(jnp.int32)
    token_level = with_ends(jax.random.randint(keys[5], (TOKENS,), 0, LEVELS), jax.random.fold_in(keys[5], 1), 0, LEVELS - 1).astype(jnp.int32)
    w_gate_up = scatter_about(keys[6], (EXPERTS, D, 2 * H), D ** -0.5, 0.09375, ((0, 32),))
    w_down = scatter_about(keys[7], (EXPERTS, H, D), H ** -0.5, 0.25, ((0, 32),))
    return {"tokens": tokens, "cotangent": cotangent, "gate_probs": gate_probs, "experts": experts, "stratum": stratum, "token_level": token_level, "w_gate_up": w_gate_up, "w_down": w_down}


def expert_grads(inputs, upstream, weight_in, weight_out):
    hidden_units = weight_out.shape[0]
    projected = jnp.dot(inputs, weight_in, preferred_element_type=jnp.float32)
    gate_part = projected[:, :hidden_units]
    up_part = projected[:, hidden_units:]
    sigmoid_gate = jax.nn.sigmoid(gate_part)
    activated = gate_part * sigmoid_gate
    hidden = (activated * up_part).astype(jnp.bfloat16)
    backward = jnp.dot(upstream, weight_out.T, preferred_element_type=jnp.float32)
    prob_grad = jnp.sum(hidden.astype(jnp.float32) * backward, axis=1).astype(jnp.bfloat16)
    grad_gate = backward * up_part * sigmoid_gate * (1.0 + gate_part * (1.0 - sigmoid_gate))
    grad_up = backward * activated
    stacked = jnp.concatenate([grad_gate, grad_up], axis=1).astype(jnp.bfloat16)
    row_grads = jnp.dot(stacked, weight_in.T, preferred_element_type=jnp.float32).astype(jnp.bfloat16)
    return row_grads, prob_grad


def reference(tokens, cotangent, gate_probs, experts, stratum, token_level, w_gate_up, w_down):
    device_count = N_NODE * N_LOCAL
    slot_count = device_count * CAP
    owner_device = jnp.arange(TOKENS, dtype=jnp.int32) // TOK_DEV
    token_stratum = stratum[owner_device]
    masked = token_level * STRATA < (token_stratum + 1) * LEVELS
    loss_weight = jnp.where(masked, STRATA / (token_stratum + 1).astype(jnp.float32), jnp.float32(0.0))
    upstream = (cotangent.astype(jnp.float32) * loss_weight[:, None]).astype(jnp.bfloat16)
    chosen = experts.reshape(-1)
    pair_count = chosen.shape[0]
    onehot = (chosen[:, None] == jnp.arange(EXPERTS, dtype=jnp.int32)[None, :]).astype(jnp.int32)
    ranking = jnp.sum((jnp.cumsum(onehot, axis=0) - 1) * onehot, axis=1)
    placed = chosen * slot_count + ranking
    owner_table = jnp.full((EXPERTS * slot_count,), pair_count, jnp.int32)
    owner_table = owner_table.at[placed].set(jnp.arange(pair_count, dtype=jnp.int32)).reshape(EXPERTS, slot_count)
    padded_tokens = jnp.concatenate([tokens, jnp.zeros((1, D), jnp.bfloat16)], axis=0)
    padded_upstream = jnp.concatenate([upstream, jnp.zeros((1, D), jnp.bfloat16)], axis=0)
    padded_probs = jnp.concatenate([gate_probs.reshape(-1), jnp.zeros((1,), jnp.float32)], axis=0)

    def per_expert(carry, pieces):
        grad_accum, prob_accum = carry
        weight_in, weight_out, pair_index = pieces
        token_index = pair_index // TOP
        row_grads, prob_grad = expert_grads(padded_tokens[token_index], padded_upstream[token_index], weight_in, weight_out)
        scaled = padded_probs[pair_index][:, None] * row_grads.astype(jnp.float32)
        grad_accum = grad_accum.at[token_index].add(scaled, mode="drop")
        prob_accum = prob_accum.at[pair_index].set(prob_grad, mode="drop")
        return (grad_accum, prob_accum), None

    start = (jnp.zeros((TOKENS, D), jnp.float32), jnp.zeros((pair_count,), jnp.bfloat16))
    (grad_accum, prob_accum), unused = lax.scan(per_expert, start, (w_gate_up, w_down, owner_table))
    return grad_accum.astype(jnp.bfloat16), prob_accum.reshape(TOKENS, TOP)
```

```python
import functools

import jax
import jax.numpy as jnp
from jax import lax
from jax.sharding import PartitionSpec as P

STRATA = 8
LEVELS = 64
BOTH = ("node", "local")
PARTS = 2


def exchange(rows):
    return lax.all_to_all(rows, "local", split_axis=0, concat_axis=0, tiled=True)


def routed(capacity, column_tokens, upstream, meta, weight_in, weight_out):
    nodes, locals_ = lax.axis_size("node"), lax.axis_size("local")
    node, local = lax.axis_index("node"), lax.axis_index("local")
    token_rows, width = upstream.shape
    chosen_count = (meta.shape[1] - 1) // 2
    expert_count = nodes * locals_
    hidden_units = weight_out.shape[0]
    column_rows = nodes * token_rows

    column = lax.dynamic_slice_in_dim(
        meta.reshape((nodes, locals_) + meta.shape[1:]), local, 1, axis=1
    )[:, 0]
    chosen = column[:, :chosen_count, :token_rows]
    probs = column[:, chosen_count : 2 * chosen_count, :token_rows]
    counts = column[:, 2 * chosen_count, :expert_count]

    plane = (node * locals_ + jnp.arange(locals_, dtype=jnp.int32)).astype(jnp.float32)
    hits = chosen[:, :, None, :] == plane[None, None, :, None]
    named = jnp.any(hits, axis=1).transpose(1, 0, 2).reshape(locals_, column_rows)
    weight = jnp.sum(jnp.where(hits, probs[:, :, None, :], 0.0), axis=1)
    weight = weight.transpose(1, 0, 2).reshape(locals_, column_rows)
    order = jnp.arange(column_rows, dtype=jnp.int32)
    before = (order[:, None] < order[None, :]).astype(jnp.bfloat16)
    slot = jnp.dot(named.astype(jnp.bfloat16), before, preferred_element_type=jnp.float32)
    slots = jnp.arange(capacity, dtype=jnp.int32).astype(jnp.float32)
    placed = named[:, None, :] & (slot[:, None, :] == slots[None, :, None])
    select = placed.astype(jnp.bfloat16).reshape(locals_ * capacity, column_rows)
    combine = (
        jnp.where(placed, weight[:, None, :], 0.0)
        .astype(jnp.bfloat16)
        .reshape(locals_ * capacity, column_rows)
    )

    def dispatch(values):
        sent = jnp.dot(select, values, preferred_element_type=jnp.float32)
        sent = sent.astype(jnp.bfloat16).reshape(locals_, capacity, width)
        return exchange(sent).reshape(locals_ * capacity, width)

    column_upstream = lax.all_gather(upstream, "node", axis=0, tiled=True)
    inputs = dispatch(column_tokens)
    projected = jnp.dot(inputs, weight_in, preferred_element_type=jnp.float32)
    gate_part = projected[:, :hidden_units]
    up_part = projected[:, hidden_units:]
    sigmoid_gate = jax.nn.sigmoid(gate_part)
    activated = gate_part * sigmoid_gate
    hidden = (activated * up_part).astype(jnp.bfloat16)

    arrived = dispatch(column_upstream)
    backward = lax.dot_general(
        arrived, weight_out, (((1,), (1,)), ((), ())), preferred_element_type=jnp.float32
    )
    prob_grad = jnp.sum(hidden.astype(jnp.float32) * backward, axis=1).astype(jnp.bfloat16)
    grad_gate = backward * up_part * sigmoid_gate * (1.0 + gate_part * (1.0 - sigmoid_gate))
    grad_up = backward * activated
    stacked = jnp.concatenate([grad_gate, grad_up], axis=1).astype(jnp.bfloat16)

    all_probs = lax.all_gather(prob_grad.reshape(locals_, capacity), BOTH, axis=0)

    piece = width // PARTS
    grads = []
    for part in range(PARTS):
        rows = lax.dot_general(
            stacked,
            weight_in[part * piece : (part + 1) * piece],
            (((1,), (1,)), ((), ())),
            preferred_element_type=jnp.float32,
        ).astype(jnp.bfloat16)
        home = exchange(rows.reshape(locals_, capacity, piece))
        partial = lax.dot_general(
            combine,
            home.reshape(locals_ * capacity, piece),
            (((0,), (0,)), ((), ())),
            preferred_element_type=jnp.float32,
        ).astype(jnp.bfloat16)
        grads.append(lax.psum_scatter(partial, "node", scatter_dimension=0, tiled=True))
    grad_tokens = jnp.concatenate(grads, axis=1)

    own = lax.dynamic_index_in_dim(chosen, node, axis=0, keepdims=False)
    every = jnp.arange(expert_count, dtype=jnp.int32).astype(jnp.float32)
    own_hits = own[None, :, :] == every[:, None, None]
    own_named = jnp.any(own_hits, axis=1)
    own_before = before[:token_rows, :token_rows]
    own_slot = jnp.dot(
        own_named.astype(jnp.bfloat16), own_before, preferred_element_type=jnp.float32
    )
    ahead = jnp.sum(
        jnp.where(jnp.arange(nodes)[:, None] < node, counts, 0.0), axis=0
    )
    own_slot = own_slot + ahead[:, None]
    mine = lax.dynamic_index_in_dim(all_probs, local, axis=1, keepdims=False)
    picked = jnp.sum(
        jnp.where(
            own_slot[:, None, :] == slots[None, :, None],
            mine.astype(jnp.float32)[:, :, None],
            0.0,
        ),
        axis=1,
    )
    grad_probs = jnp.sum(jnp.where(own_hits, picked[:, None, :], 0.0), axis=0)
    return grad_tokens, grad_probs.T.astype(jnp.bfloat16)


def body(tokens, cotangent, gate_probs, experts, stratum, token_level, w_gate_up, w_down):
    nodes, locals_ = lax.axis_size("node"), lax.axis_size("local")
    expert_count = nodes * locals_
    token_rows, chosen_count = experts.shape
    capacity = max(2, token_rows * chosen_count * 5 // (4 * expert_count))
    stratum_here = stratum[0]
    masked = token_level * STRATA < (stratum_here + 1) * LEVELS
    loss_weight = jnp.where(
        masked, STRATA / (stratum_here + 1).astype(jnp.float32), jnp.float32(0.0)
    )
    upstream = (cotangent.astype(jnp.float32) * loss_weight[:, None]).astype(jnp.bfloat16)

    chosen = jnp.where(masked[:, None], experts, -1).T
    every = jnp.arange(expert_count, dtype=jnp.int32)
    counts = jnp.sum(
        (chosen[:, :, None] == every[None, None, :]).astype(jnp.float32), axis=(0, 1)
    )[None, :]
    lanes = max(token_rows, expert_count)

    def wide(rows):
        return jnp.pad(rows, ((0, 0), (0, lanes - rows.shape[1])))

    meta = jnp.concatenate(
        [wide(chosen.astype(jnp.float32)), wide(gate_probs.T), wide(counts)], axis=0
    )
    meta = lax.all_gather(meta, BOTH, axis=0)
    column_tokens = lax.all_gather(tokens, "node", axis=0, tiled=True)

    needed = jnp.max(
        jnp.sum(meta[:, 2 * chosen_count, :].reshape(nodes, locals_, lanes), axis=0)
    )
    most = nodes * capacity
    sizes = sorted({max(16, most * part // 160 // 16 * 16) for part in (96, 112, 128, 144)})
    sizes = [size for size in sizes if size < most] + [most]
    which = jnp.sum(
        (needed > jnp.array(sizes[:-1], jnp.float32)).astype(jnp.int32)
    )
    return lax.switch(
        which,
        [functools.partial(routed, size) for size in sizes],
        column_tokens,
        upstream,
        meta,
        w_gate_up[0],
        w_down[0],
    )


def solution(mesh):
    placed = (
        P(BOTH, None),
        P(BOTH, None),
        P(BOTH, None),
        P(BOTH, None),
        P(BOTH),
        P(BOTH),
        P(BOTH, None, None),
        P(BOTH, None, None),
    )
    return jax.shard_map(
        body,
        mesh=mesh,
        in_specs=placed,
        out_specs=(P(BOTH, None), P(BOTH, None)),
        check_vma=False,
    )
```

```python
import functools

import jax
import jax.numpy as jnp
from jax import lax
from jax.sharding import PartitionSpec as P

STRATA = 8
LEVELS = 64
BOTH = ("node", "local")
PARTS = 2
LANES = 128


def exchange(rows):
    return lax.all_to_all(rows, "local", split_axis=0, concat_axis=0, tiled=True)


def routed(capacity, first_tokens, tokens, upstream, meta, weight_in, weight_out):
    nodes, locals_ = lax.axis_size("node"), lax.axis_size("local")
    node, local = lax.axis_index("node"), lax.axis_index("local")
    token_rows, width = upstream.shape
    chosen_count = (meta.shape[1] - 1) // 2
    hidden_units = weight_out.shape[0]
    column_rows = nodes * token_rows

    column = lax.dynamic_slice_in_dim(
        meta.reshape((nodes, locals_) + meta.shape[1:]), local, 1, axis=1
    )[:, 0]
    chosen = column[:, :chosen_count, :token_rows]
    probs = column[:, chosen_count : 2 * chosen_count, :token_rows]

    plane = (node * locals_ + jnp.arange(locals_, dtype=jnp.int32)).astype(jnp.float32)
    hits = chosen[:, :, None, :] == plane[None, None, :, None]
    named = jnp.any(hits, axis=1).transpose(1, 0, 2).reshape(locals_, column_rows)
    weight = jnp.sum(jnp.where(hits, probs[:, :, None, :], 0.0), axis=1)
    weight = weight.transpose(1, 0, 2).reshape(locals_, column_rows)
    order = jnp.arange(column_rows, dtype=jnp.int32)
    before = (order[:, None] < order[None, :]).astype(jnp.bfloat16)
    slot = jnp.dot(named.astype(jnp.bfloat16), before, preferred_element_type=jnp.float32)
    slots = jnp.arange(capacity, dtype=jnp.int32).astype(jnp.float32)
    placed = named[:, None, :] & (slot[:, None, :] == slots[None, :, None])
    select = placed.astype(jnp.bfloat16).reshape(locals_ * capacity, column_rows)
    combine = (
        jnp.where(placed, weight[:, None, :], 0.0)
        .astype(jnp.bfloat16)
        .reshape(locals_ * capacity, column_rows)
    )

    def dispatch(values):
        sent = jnp.dot(select, values, preferred_element_type=jnp.float32)
        sent = sent.astype(jnp.bfloat16).reshape(locals_, capacity, values.shape[1])
        return exchange(sent).reshape(locals_ * capacity, values.shape[1])

    piece = width // PARTS
    cuts = [slice(part * piece, (part + 1) * piece) for part in range(PARTS)]
    later = [lax.all_gather(tokens[:, cut], "node", axis=0, tiled=True) for cut in cuts[1:]]
    column_upstream = [
        lax.all_gather(upstream[:, cut], "node", axis=0, tiled=True) for cut in cuts
    ]
    projected = 0.0
    for cut, values in zip(cuts, [first_tokens] + later):
        projected = projected + jnp.dot(
            dispatch(values), weight_in[cut], preferred_element_type=jnp.float32
        )
    gate_part = projected[:, :hidden_units]
    up_part = projected[:, hidden_units:]
    sigmoid_gate = jax.nn.sigmoid(gate_part)
    activated = gate_part * sigmoid_gate
    hidden = (activated * up_part).astype(jnp.bfloat16)

    backward = 0.0
    for cut, values in zip(cuts, column_upstream):
        backward = backward + lax.dot_general(
            dispatch(values),
            weight_out[:, cut],
            (((1,), (1,)), ((), ())),
            preferred_element_type=jnp.float32,
        )
    prob_grad = jnp.sum(hidden.astype(jnp.float32) * backward, axis=1).astype(jnp.bfloat16)
    grad_gate = backward * up_part * sigmoid_gate * (1.0 + gate_part * (1.0 - sigmoid_gate))
    grad_up = backward * activated
    stacked = jnp.concatenate([grad_gate, grad_up], axis=1).astype(jnp.bfloat16)

    grads = []
    for part, cut in enumerate(cuts):
        rows = lax.dot_general(
            stacked, weight_in[cut], (((1,), (1,)), ((), ())), preferred_element_type=jnp.float32
        ).astype(jnp.bfloat16)
        if part == 0:
            column_of = jnp.pad(prob_grad[:, None], ((0, 0), (0, LANES - 1)))
            rows = jnp.concatenate([rows, column_of], axis=1)
        home = exchange(rows.reshape(locals_, capacity, rows.shape[1]))
        partial = lax.dot_general(
            combine,
            home[:, :, :piece].reshape(locals_ * capacity, piece),
            (((0,), (0,)), ((), ())),
            preferred_element_type=jnp.float32,
        ).astype(jnp.bfloat16)
        if part == 0:
            home_probs = home[:, :, piece].astype(jnp.float32)
            by_expert = jnp.sum(jnp.where(placed, home_probs[:, :, None], 0.0), axis=1)
            by_expert = by_expert.reshape(locals_, nodes, token_rows).transpose(1, 0, 2)
            by_choice = jnp.sum(jnp.where(hits, by_expert[:, None, :, :], 0.0), axis=2)
            by_choice = by_choice.transpose(0, 2, 1).reshape(column_rows, chosen_count)
            by_choice = jnp.pad(by_choice, ((0, 0), (0, LANES - chosen_count)))
            partial = jnp.concatenate([partial, by_choice.astype(jnp.bfloat16)], axis=1)
        grads.append(lax.psum_scatter(partial, "node", scatter_dimension=0, tiled=True))
    grad_probs = grads[0][:, piece : piece + chosen_count]
    grads[0] = grads[0][:, :piece]
    return jnp.concatenate(grads, axis=1), grad_probs


def body(tokens, cotangent, gate_probs, experts, stratum, token_level, w_gate_up, w_down):
    nodes, locals_ = lax.axis_size("node"), lax.axis_size("local")
    expert_count = nodes * locals_
    token_rows, chosen_count = experts.shape
    capacity = max(2, token_rows * chosen_count * 5 // (4 * expert_count))
    stratum_here = stratum[0]
    masked = token_level * STRATA < (stratum_here + 1) * LEVELS
    loss_weight = jnp.where(
        masked, STRATA / (stratum_here + 1).astype(jnp.float32), jnp.float32(0.0)
    )
    upstream = (cotangent.astype(jnp.float32) * loss_weight[:, None]).astype(jnp.bfloat16)

    chosen = jnp.where(masked[:, None], experts, -1).T
    every = jnp.arange(expert_count, dtype=jnp.int32)
    counts = jnp.sum(
        (chosen[:, :, None] == every[None, None, :]).astype(jnp.float32), axis=(0, 1)
    )[None, :]
    lanes = max(token_rows, expert_count)

    def wide(rows):
        return jnp.pad(rows, ((0, 0), (0, lanes - rows.shape[1])))

    meta = jnp.concatenate(
        [wide(chosen.astype(jnp.float32)), wide(gate_probs.T), wide(counts)], axis=0
    )
    meta = lax.all_to_all(
        jnp.broadcast_to(meta[None], (expert_count,) + meta.shape),
        BOTH,
        split_axis=0,
        concat_axis=0,
        tiled=True,
    )
    first_tokens = lax.all_gather(
        tokens[:, : tokens.shape[1] // PARTS], "node", axis=0, tiled=True
    )

    needed = jnp.max(
        jnp.sum(meta[:, 2 * chosen_count, :].reshape(nodes, locals_, lanes), axis=0)
    )
    most = nodes * capacity
    sizes = sorted({max(8, most * part // 20 // 8 * 8) for part in range(11, 20)})
    sizes = [size for size in sizes if size < most] + [most]
    which = jnp.sum(
        (needed > jnp.array(sizes[:-1], jnp.float32)).astype(jnp.int32)
    )
    return lax.switch(
        which,
        [functools.partial(routed, size) for size in sizes],
        first_tokens,
        tokens,
        upstream,
        meta,
        w_gate_up[0],
        w_down[0],
    )


def solution(mesh):
    placed = (
        P(BOTH, None),
        P(BOTH, None),
        P(BOTH, None),
        P(BOTH, None),
        P(BOTH),
        P(BOTH),
        P(BOTH, None, None),
        P(BOTH, None, None),
    )
    return jax.shard_map(
        body,
        mesh=mesh,
        in_specs=placed,
        out_specs=(P(BOTH, None), P(BOTH, None)),
        check_vma=False,
    )
```

```python
import functools

import jax
import jax.numpy as jnp
from jax import lax
from jax.sharding import PartitionSpec as P

STRATA = 8
LEVELS = 64
BOTH = ("node", "local")
TOKEN_PIECES = (2, 2, 4)
UPSTREAM_PIECES = (4, 4)
RETURN_PIECES = (3, 3, 2)
LANES = 128


def columns(width, pieces):
    starts = [sum(pieces[:part]) * width // 8 for part in range(len(pieces) + 1)]
    return [slice(start, stop) for start, stop in zip(starts, starts[1:])]


def exchange(rows):
    return lax.all_to_all(rows, "local", split_axis=0, concat_axis=0, tiled=True)


def routed(capacity, first_tokens, tokens, upstream, meta, weight_in, weight_out):
    nodes, locals_ = lax.axis_size("node"), lax.axis_size("local")
    node, local = lax.axis_index("node"), lax.axis_index("local")
    token_rows, width = upstream.shape
    chosen_count = (meta.shape[1] - 1) // 2
    hidden_units = weight_out.shape[0]
    column_rows = nodes * token_rows

    column = lax.dynamic_slice_in_dim(
        meta.reshape((nodes, locals_) + meta.shape[1:]), local, 1, axis=1
    )[:, 0]
    chosen = column[:, :chosen_count, :token_rows]
    probs = column[:, chosen_count : 2 * chosen_count, :token_rows]

    plane = (node * locals_ + jnp.arange(locals_, dtype=jnp.int32)).astype(jnp.float32)
    hits = chosen[:, :, None, :] == plane[None, None, :, None]
    named = jnp.any(hits, axis=1).transpose(1, 0, 2).reshape(locals_, column_rows)
    weight = jnp.sum(jnp.where(hits, probs[:, :, None, :], 0.0), axis=1)
    weight = weight.transpose(1, 0, 2).reshape(locals_, column_rows)
    order = jnp.arange(column_rows, dtype=jnp.int32)
    before = (order[:, None] < order[None, :]).astype(jnp.bfloat16)
    slot = jnp.dot(named.astype(jnp.bfloat16), before, preferred_element_type=jnp.float32)
    slots = jnp.arange(capacity, dtype=jnp.int32).astype(jnp.float32)
    placed = named[:, None, :] & (slot[:, None, :] == slots[None, :, None])
    select = placed.astype(jnp.bfloat16).reshape(locals_ * capacity, column_rows)
    combine = (
        jnp.where(placed, weight[:, None, :], 0.0)
        .astype(jnp.bfloat16)
        .reshape(locals_ * capacity, column_rows)
    )

    def dispatch(values):
        sent = jnp.dot(select, values, preferred_element_type=jnp.float32)
        sent = sent.astype(jnp.bfloat16).reshape(locals_, capacity, values.shape[1])
        return exchange(sent).reshape(locals_ * capacity, values.shape[1])

    token_cuts = columns(width, TOKEN_PIECES)
    upstream_cuts = columns(width, UPSTREAM_PIECES)
    column_tokens = [first_tokens] + [
        lax.all_gather(tokens[:, cut], "node", axis=0, tiled=True) for cut in token_cuts[1:]
    ]
    column_upstream = [
        lax.all_gather(upstream[:, cut], "node", axis=0, tiled=True) for cut in upstream_cuts
    ]
    projected = 0.0
    for cut, values in zip(token_cuts, column_tokens):
        projected = projected + jnp.dot(
            dispatch(values), weight_in[cut], preferred_element_type=jnp.float32
        )
    gate_part = projected[:, :hidden_units]
    up_part = projected[:, hidden_units:]
    sigmoid_gate = jax.nn.sigmoid(gate_part)
    activated = gate_part * sigmoid_gate
    hidden = (activated * up_part).astype(jnp.bfloat16)

    backward = 0.0
    for cut, values in zip(upstream_cuts, column_upstream):
        backward = backward + lax.dot_general(
            dispatch(values),
            weight_out[:, cut],
            (((1,), (1,)), ((), ())),
            preferred_element_type=jnp.float32,
        )
    prob_grad = jnp.sum(hidden.astype(jnp.float32) * backward, axis=1).astype(jnp.bfloat16)
    grad_gate = backward * up_part * sigmoid_gate * (1.0 + gate_part * (1.0 - sigmoid_gate))
    grad_up = backward * activated
    stacked = jnp.concatenate([grad_gate, grad_up], axis=1).astype(jnp.bfloat16)

    grads = []
    for part, cut in enumerate(columns(width, RETURN_PIECES)):
        piece = cut.stop - cut.start
        rows = lax.dot_general(
            stacked, weight_in[cut], (((1,), (1,)), ((), ())), preferred_element_type=jnp.float32
        ).astype(jnp.bfloat16)
        if part == 0:
            column_of = jnp.pad(prob_grad[:, None], ((0, 0), (0, LANES - 1)))
            rows = jnp.concatenate([rows, column_of], axis=1)
        home = exchange(rows.reshape(locals_, capacity, rows.shape[1]))
        partial = lax.dot_general(
            combine,
            home[:, :, :piece].reshape(locals_ * capacity, piece),
            (((0,), (0,)), ((), ())),
            preferred_element_type=jnp.float32,
        ).astype(jnp.bfloat16)
        if part == 0:
            home_probs = home[:, :, piece].astype(jnp.float32)
            by_expert = jnp.sum(jnp.where(placed, home_probs[:, :, None], 0.0), axis=1)
            by_expert = by_expert.reshape(locals_, nodes, token_rows).transpose(1, 0, 2)
            by_choice = jnp.sum(jnp.where(hits, by_expert[:, None, :, :], 0.0), axis=2)
            by_choice = by_choice.transpose(0, 2, 1).reshape(column_rows, chosen_count)
            by_choice = jnp.pad(by_choice, ((0, 0), (0, LANES - chosen_count)))
            partial = jnp.concatenate([partial, by_choice.astype(jnp.bfloat16)], axis=1)
        grads.append(lax.psum_scatter(partial, "node", scatter_dimension=0, tiled=True))
    piece = RETURN_PIECES[0] * width // 8
    grad_probs = grads[0][:, piece : piece + chosen_count]
    grads[0] = grads[0][:, :piece]
    return jnp.concatenate(grads, axis=1), grad_probs


def body(tokens, cotangent, gate_probs, experts, stratum, token_level, w_gate_up, w_down):
    nodes, locals_ = lax.axis_size("node"), lax.axis_size("local")
    expert_count = nodes * locals_
    token_rows, chosen_count = experts.shape
    capacity = max(2, token_rows * chosen_count * 5 // (4 * expert_count))
    stratum_here = stratum[0]
    masked = token_level * STRATA < (stratum_here + 1) * LEVELS
    loss_weight = jnp.where(
        masked, STRATA / (stratum_here + 1).astype(jnp.float32), jnp.float32(0.0)
    )
    upstream = (cotangent.astype(jnp.float32) * loss_weight[:, None]).astype(jnp.bfloat16)

    chosen = jnp.where(masked[:, None], experts, -1).T
    every = jnp.arange(expert_count, dtype=jnp.int32)
    counts = jnp.sum(
        (chosen[:, :, None] == every[None, None, :]).astype(jnp.float32), axis=(0, 1)
    )[None, :]
    lanes = max(token_rows, expert_count)

    def wide(rows):
        return jnp.pad(rows, ((0, 0), (0, lanes - rows.shape[1])))

    meta = jnp.concatenate(
        [wide(chosen.astype(jnp.float32)), wide(gate_probs.T), wide(counts)], axis=0
    )
    meta = lax.all_to_all(
        jnp.broadcast_to(meta[None], (expert_count,) + meta.shape),
        BOTH,
        split_axis=0,
        concat_axis=0,
        tiled=True,
    )
    first_tokens = lax.all_gather(
        tokens[:, columns(tokens.shape[1], TOKEN_PIECES)[0]], "node", axis=0, tiled=True
    )

    needed = jnp.max(
        jnp.sum(meta[:, 2 * chosen_count, :].reshape(nodes, locals_, lanes), axis=0)
    )
    most = nodes * capacity
    sizes = sorted({max(8, most * part // 20 // 8 * 8) for part in (15, 18)})
    sizes = [size for size in sizes if size < most] + [most]
    which = jnp.sum(
        (needed > jnp.array(sizes[:-1], jnp.float32)).astype(jnp.int32)
    )
    return lax.switch(
        which,
        [functools.partial(routed, size) for size in sizes],
        first_tokens,
        tokens,
        upstream,
        meta,
        w_gate_up[0],
        w_down[0],
    )


def solution(mesh):
    placed = (
        P(BOTH, None),
        P(BOTH, None),
        P(BOTH, None),
        P(BOTH, None),
        P(BOTH),
        P(BOTH),
        P(BOTH, None, None),
        P(BOTH, None, None),
    )
    return jax.shard_map(
        body,
        mesh=mesh,
        in_specs=placed,
        out_specs=(P(BOTH, None), P(BOTH, None)),
        check_vma=False,
    )
```

```python
import functools

import jax
import jax.numpy as jnp
from jax import lax
from jax.sharding import PartitionSpec as P

STRATA = 8
LEVELS = 64
BOTH = ("node", "local")
TOKEN_PIECES = (4, 4)
UPSTREAM_PIECES = (4, 4)
RETURN_PIECES = (3, 3, 2)
LANES = 128


def columns(width, pieces):
    starts = [sum(pieces[:part]) * width // 8 for part in range(len(pieces) + 1)]
    return [slice(start, stop) for start, stop in zip(starts, starts[1:])]


def exchange(rows):
    return lax.all_to_all(rows, "local", split_axis=0, concat_axis=0, tiled=True)


def routed(capacity, first_tokens, tokens, upstream, meta, weight_in, weight_out):
    nodes, locals_ = lax.axis_size("node"), lax.axis_size("local")
    node, local = lax.axis_index("node"), lax.axis_index("local")
    token_rows, width = upstream.shape
    chosen_count = (meta.shape[1] - 1) // 2
    hidden_units = weight_out.shape[0]
    column_rows = nodes * token_rows

    column = lax.dynamic_slice_in_dim(
        meta.reshape((nodes, locals_) + meta.shape[1:]), local, 1, axis=1
    )[:, 0]
    chosen = column[:, :chosen_count, :token_rows]
    probs = column[:, chosen_count : 2 * chosen_count, :token_rows]

    plane = (node * locals_ + jnp.arange(locals_, dtype=jnp.int32)).astype(jnp.float32)
    hits = chosen[:, :, None, :] == plane[None, None, :, None]
    named = jnp.any(hits, axis=1).transpose(1, 0, 2).reshape(locals_, column_rows)
    weight = jnp.sum(jnp.where(hits, probs[:, :, None, :], 0.0), axis=1)
    weight = weight.transpose(1, 0, 2).reshape(locals_, column_rows)
    order = jnp.arange(column_rows, dtype=jnp.int32)
    before = (order[:, None] < order[None, :]).astype(jnp.bfloat16)
    slot = jnp.dot(named.astype(jnp.bfloat16), before, preferred_element_type=jnp.float32)
    slots = jnp.arange(capacity, dtype=jnp.int32).astype(jnp.float32)
    placed = named[:, None, :] & (slot[:, None, :] == slots[None, :, None])
    select = placed.astype(jnp.bfloat16).reshape(locals_ * capacity, column_rows)
    combine = (
        jnp.where(placed, weight[:, None, :], 0.0)
        .astype(jnp.bfloat16)
        .reshape(locals_ * capacity, column_rows)
    )

    def dispatch(values):
        sent = jnp.dot(select, values, preferred_element_type=jnp.float32)
        sent = sent.astype(jnp.bfloat16).reshape(locals_, capacity, values.shape[1])
        return exchange(sent).reshape(locals_ * capacity, values.shape[1])

    token_cuts = columns(width, TOKEN_PIECES)
    upstream_cuts = columns(width, UPSTREAM_PIECES)
    column_tokens = [first_tokens] + [
        lax.all_gather(tokens[:, cut], "node", axis=0, tiled=True) for cut in token_cuts[1:]
    ]
    column_upstream = [
        lax.all_gather(upstream[:, cut], "node", axis=0, tiled=True) for cut in upstream_cuts
    ]
    projected = 0.0
    for cut, values in zip(token_cuts, column_tokens):
        projected = projected + jnp.dot(
            dispatch(values), weight_in[cut], preferred_element_type=jnp.float32
        )
    gate_part = projected[:, :hidden_units]
    up_part = projected[:, hidden_units:]
    sigmoid_gate = jax.nn.sigmoid(gate_part)
    activated = gate_part * sigmoid_gate
    hidden = (activated * up_part).astype(jnp.bfloat16)

    backward = 0.0
    for cut, values in zip(upstream_cuts, column_upstream):
        backward = backward + lax.dot_general(
            dispatch(values),
            weight_out[:, cut],
            (((1,), (1,)), ((), ())),
            preferred_element_type=jnp.float32,
        )
    prob_grad = jnp.sum(hidden.astype(jnp.float32) * backward, axis=1).astype(jnp.bfloat16)
    grad_gate = backward * up_part * sigmoid_gate * (1.0 + gate_part * (1.0 - sigmoid_gate))
    grad_up = backward * activated
    stacked = jnp.concatenate([grad_gate, grad_up], axis=1).astype(jnp.bfloat16)

    grads = []
    for part, cut in enumerate(columns(width, RETURN_PIECES)):
        piece = cut.stop - cut.start
        rows = lax.dot_general(
            stacked, weight_in[cut], (((1,), (1,)), ((), ())), preferred_element_type=jnp.float32
        ).astype(jnp.bfloat16)
        if part == 0:
            column_of = jnp.pad(prob_grad[:, None], ((0, 0), (0, LANES - 1)))
            rows = jnp.concatenate([rows, column_of], axis=1)
        if part > 0:
            rows, home = lax.optimization_barrier((rows, home))
        home = exchange(rows.reshape(locals_, capacity, rows.shape[1]))
        partial = lax.dot_general(
            combine,
            home[:, :, :piece].reshape(locals_ * capacity, piece),
            (((0,), (0,)), ((), ())),
            preferred_element_type=jnp.float32,
        ).astype(jnp.bfloat16)
        if part == 0:
            home_probs = home[:, :, piece].astype(jnp.float32)
            by_expert = jnp.sum(jnp.where(placed, home_probs[:, :, None], 0.0), axis=1)
            by_expert = by_expert.reshape(locals_, nodes, token_rows).transpose(1, 0, 2)
            by_choice = jnp.sum(jnp.where(hits, by_expert[:, None, :, :], 0.0), axis=2)
            by_choice = by_choice.transpose(0, 2, 1).reshape(column_rows, chosen_count)
            by_choice = jnp.pad(by_choice, ((0, 0), (0, LANES - chosen_count)))
            partial = jnp.concatenate([partial, by_choice.astype(jnp.bfloat16)], axis=1)
        grads.append(lax.psum_scatter(partial, "node", scatter_dimension=0, tiled=True))
    piece = RETURN_PIECES[0] * width // 8
    grad_probs = grads[0][:, piece : piece + chosen_count]
    grads[0] = grads[0][:, :piece]
    return jnp.concatenate(grads, axis=1), grad_probs


def body(tokens, cotangent, gate_probs, experts, stratum, token_level, w_gate_up, w_down):
    nodes, locals_ = lax.axis_size("node"), lax.axis_size("local")
    expert_count = nodes * locals_
    token_rows, chosen_count = experts.shape
    capacity = max(2, token_rows * chosen_count * 5 // (4 * expert_count))
    stratum_here = stratum[0]
    masked = token_level * STRATA < (stratum_here + 1) * LEVELS
    loss_weight = jnp.where(
        masked, STRATA / (stratum_here + 1).astype(jnp.float32), jnp.float32(0.0)
    )
    upstream = (cotangent.astype(jnp.float32) * loss_weight[:, None]).astype(jnp.bfloat16)

    chosen = jnp.where(masked[:, None], experts, -1).T
    every = jnp.arange(expert_count, dtype=jnp.int32)
    counts = jnp.sum(
        (chosen[:, :, None] == every[None, None, :]).astype(jnp.float32), axis=(0, 1)
    )[None, :]
    lanes = max(token_rows, expert_count)

    def wide(rows):
        return jnp.pad(rows, ((0, 0), (0, lanes - rows.shape[1])))

    meta = jnp.concatenate(
        [wide(chosen.astype(jnp.float32)), wide(gate_probs.T), wide(counts)], axis=0
    )
    meta = lax.all_to_all(
        jnp.broadcast_to(meta[None], (expert_count,) + meta.shape),
        BOTH,
        split_axis=0,
        concat_axis=0,
        tiled=True,
    )
    first_tokens = lax.all_gather(
        tokens[:, columns(tokens.shape[1], TOKEN_PIECES)[0]], "node", axis=0, tiled=True
    )

    needed = jnp.max(
        jnp.sum(meta[:, 2 * chosen_count, :].reshape(nodes, locals_, lanes), axis=0)
    )
    most = nodes * capacity
    sizes = sorted({max(8, most * part // 20 // 8 * 8) for part in (15, 18)})
    sizes = [size for size in sizes if size < most] + [most]
    which = jnp.sum(
        (needed > jnp.array(sizes[:-1], jnp.float32)).astype(jnp.int32)
    )
    return lax.switch(
        which,
        [functools.partial(routed, size) for size in sizes],
        first_tokens,
        tokens,
        upstream,
        meta,
        w_gate_up[0],
        w_down[0],
    )


def solution(mesh):
    placed = (
        P(BOTH, None),
        P(BOTH, None),
        P(BOTH, None),
        P(BOTH, None),
        P(BOTH),
        P(BOTH),
        P(BOTH, None, None),
        P(BOTH, None, None),
    )
    return jax.shard_map(
        body,
        mesh=mesh,
        in_specs=placed,
        out_specs=(P(BOTH, None), P(BOTH, None)),
        check_vma=False,
    )
```
